256 devices in a mesh: prow: 16 (over z, y_lo), pcol: 16 (over x, y_hi, core).
Axes of the slice: x: 4, y: 4 (y_hi: 2, y_lo: 2; y = y_hi * 2 + y_lo), z: 8, core: 2. Of those that a mesh axis runs over, the one named last changes fastest.
Arguments:
- ainv: bfloat16 [16384, 16384], P('prow', 'pcol'), may hold values from -6 to 6
- l_panels: bfloat16 [16, 16384, 256], P('pcol', 'prow'), may hold values from -0.046875 to 0.046875
- dinv: float32 [16, 256, 256], P('pcol'), may hold values from -6 to 6
- ancestors: int32 [16, 64], replicated, may hold values from 0 to 127, as said below
- block_slot: int32 [128], replicated, may hold values from 0 to 127, each once
Outputs:
- inverse_column: bfloat16 [16, 16384, 256], P('pcol', 'prow')
- diagonal_block: float32 [16, 256, 256], P('pcol')
The draws below stay inside these ranges and needn't reach their ends.
Inputs may be any that keep to these rules, and one draw needn't show every extreme that they name: `ancestors`: each row holds 64 distinct block numbers.
All inputs are finite; a program needn't handle non-finite values.
Results may differ from the reference program's by a relative error of at most 0.0095.
Values may be sent and summed in bfloat16 or wider, within the bound.
No kernel may reach another device: no remote copies, remote signals or barrier semaphores. Data moves between devices by JAX's collectives and lax.ppermute only.
A program may use at most 128 MiB of HBM per device.

```python
import jax
import jax.numpy as jnp

W = 256
BS = 128
NSUP = 16
NB = 128
NA = 64
M = 16384


def draw_ancestors(key, part):
    key = jax.random.fold_in(key, 7)
    row_keys = jax.random.split(key, NSUP)

    def one_row(row_key):
        inner = jax.random.permutation(row_key, NB - 2)[:NA - 2].astype(jnp.int32) + 1
        first = jnp.zeros((1,), jnp.int32)
        last = jnp.full((1,), NB - 1, jnp.int32)
        return jnp.concatenate([first, inner, last])
    return jax.vmap(one_row)(row_keys).astype(jnp.int32)


def block_scale(own_key, dims, shards, least, top_value):
    def one(axis_at, shards_of):
        heights = jax.random.uniform(jax.random.fold_in(jax.random.fold_in(own_key, 6), axis_at), (shards_of,), jnp.float32, least / len(shards), top_value / len(shards))
        return jnp.repeat(jnp.exp(heights), dims[axis_at] // shards_of).reshape((-1,) + (1,) * (len(dims) - axis_at - 1))

    loudness = one(*shards[0])
    for cut in shards[1:]:
        loudness = loudness * one(*cut)
    return loudness


def noise(own_key, dims, spread, bound, cuts=(), held_as=jnp.bfloat16):
    entries = spread * jax.random.normal(own_key, dims, jnp.float32)
    if cuts:
        entries = entries * block_scale(own_key, dims, cuts, -0.22, 0.18)
    return jnp.clip(entries, -bound, bound).astype(held_as)


def setup_inputs(seed: int = 0) -> dict:
    key_list = jax.random.split(jax.random.key(seed), 6)
    ainv = noise(key_list[0], (M, M), 1.0, 6.0, ((0, 16), (1, 16)))
    l_panels = noise(key_list[1], (NSUP, M, W), M ** -0.5, 0.046875, ((0, 16), (1, 16)))
    dinv = noise(key_list[2], (NSUP, W, W), 1.0, 6.0, ((0, 16),), jnp.float32)
    ancestors = draw_ancestors(jax.random.fold_in(key_list[5], 71), 0)
    block_slot = jax.random.permutation(key_list[4], NB).astype(jnp.int32)
    return dict(ainv=ainv, l_panels=l_panels, dinv=dinv, ancestors=ancestors, block_slot=block_slot)


def membership(ancestors, block_slot):
    numbers = jnp.arange(block_slot.shape[0], dtype=jnp.int32)
    chosen = (ancestors[:, :, None] == numbers[None, None, :]).astype(jnp.int32)
    slots_used = jnp.sum(chosen * block_slot[None, None, :], axis=2)
    present = jnp.any(slots_used[:, :, None] == numbers[None, None, :], axis=1)
    return jnp.repeat(present, BS, axis=1)


def reference(ainv, l_panels, dinv, ancestors, block_slot):
    row_flags = membership(ancestors, block_slot)
    masked = jnp.where(row_flags[:, :, None], l_panels, jnp.zeros((), l_panels.dtype))
    stacked = jnp.transpose(masked, (1, 0, 2)).reshape(M, NSUP * W)
    product = jnp.dot(ainv, stacked, preferred_element_type=jnp.float32)
    product = jnp.transpose(product.reshape(M, NSUP, W), (1, 0, 2))
    inverse_column = jnp.where(row_flags[:, :, None], -product, jnp.zeros((), product.dtype)).astype(jnp.bfloat16)
    terms = jnp.einsum("kiw,kiv->kwv", masked.astype(jnp.float32), inverse_column.astype(jnp.float32))
    diagonal_block = dinv - terms
    return inverse_column, diagonal_block
```

```python
import functools

import jax
import jax.numpy as jnp
from jax import lax
from jax.experimental import pallas as pl
from jax.experimental.pallas import tpu as pltpu
from jax.sharding import PartitionSpec as P

BS = 128
NZ, NY_LO, NX, NY_HI, NCORE = 8, 2, 4, 2, 2
F32, BF16 = jnp.float32, jnp.bfloat16
AXES = ("prow", "pcol")


def device_index(z, ylo, x, yhi, core):
    return (2 * z + ylo) * 16 + 4 * x + 2 * yhi + core


def permutation(target):
    pairs = []
    for z in range(NZ):
        for ylo in range(NY_LO):
            for x in range(NX):
                for yhi in range(NY_HI):
                    for core in range(NCORE):
                        to = target(z, ylo, x, yhi, core)
                        if to is not None:
                            pairs.append((device_index(z, ylo, x, yhi, core), device_index(*to)))
    return pairs


L_TURN = permutation(lambda z, l, x, q, c: (2 * x + z % 2, c, z // 2, q, l))
Z_UP = permutation(lambda z, l, x, q, c: ((z + 1) % 8, l, x, q, c))
Z_DOWN = permutation(lambda z, l, x, q, c: ((z - 1) % 8, l, x, q, c))
Y_NEAR = permutation(lambda z, l, x, q, c: (z, 1 - l, x, q, c))
Y_FAR = permutation(lambda z, l, x, q, c: (z, 1 - l, x, 1 - q, c))
CORE = permutation(lambda z, l, x, q, c: (z, l, x, q, 1 - c))
X_UP = permutation(lambda z, l, x, q, c: (z, l, (x + 1) % 4, q, c))
X_DOWN = permutation(lambda z, l, x, q, c: (z, l, (x - 1) % 4, q, c))
HOME = permutation(lambda z, l, x, q, c: (z, c, x, q, l))


def z_swap(bit):
    return permutation(lambda z, l, x, q, c: (z ^ bit, l, x, q, c))


def move(value, pairs):
    return lax.ppermute(value, AXES, pairs)


def local_flags(ancestors, block_slot, row, column):
    own = lax.dynamic_index_in_dim(ancestors, column, 0, keepdims=False)
    numbers = jnp.arange(block_slot.shape[0], dtype=jnp.int32)
    used = jnp.any(own[:, None] == numbers[None, :], axis=0)
    slots = row * 8 + jnp.arange(8, dtype=jnp.int32)
    return jnp.any(used[None, :] & (block_slot[None, :] == slots[:, None]), axis=1)


def product_kernel(scalars, a0, a1, l0, l1, out):
    total = jnp.dot(a0[0], l0[0], preferred_element_type=F32)
    total += jnp.dot(a1[0], l1[0], preferred_element_type=F32)
    out[0] = total.astype(out.dtype)


def products(scalars, a_blocks, l_blocks, dtype):
    def l_map(flip):
        return lambda j, s: (2 * ((s[2] + j) % 4) + (s[1] ^ flip), 0, 0)

    return pl.pallas_call(
        product_kernel,
        grid_spec=pltpu.PrefetchScalarGridSpec(
            num_scalar_prefetch=1,
            grid=(4,),
            in_specs=[
                pl.BlockSpec((1, 1024, 1024), lambda j, s: (s[0], 0, 0)),
                pl.BlockSpec((1, 1024, 1024), lambda j, s: (s[0] + 1, 0, 0)),
                pl.BlockSpec((1, 1024, 256), l_map(0)),
                pl.BlockSpec((1, 1024, 256), l_map(1)),
            ],
            out_specs=pl.BlockSpec((1, 1024, 256), lambda j, s: (j, 0, 0)),
        ),
        out_shape=jax.ShapeDtypeStruct((4, 1024, 256), dtype),
        compiler_params=pltpu.CompilerParams(vmem_limit_bytes=40 * 2**20),
        cost_estimate=pl.CostEstimate(flops=2 * 1024 * 2048 * 1024, bytes_accessed=12 * 2**20, transcendentals=0),
    )(scalars, a_blocks, a_blocks, l_blocks, l_blocks)


def body(ainv, l_panels, dinv, ancestors, block_slot):
    row = lax.axis_index("prow")
    column = lax.axis_index("pcol")
    z, ylo = row // 2, row % 2
    x, yhi, core = column // 4, (column // 2) % 2, column % 2

    flags = jnp.repeat(local_flags(ancestors, block_slot, row, column), BS)[:, None]
    masked = jnp.where(flags, l_panels[0], jnp.zeros((), BF16))

    here = move(masked, L_TURN)
    near = move(ainv, Y_NEAR)
    far = move(ainv, Y_FAR)

    l_all = jnp.zeros((8, 1024, 256), BF16)
    put = lambda buffer, block, at, start=0: lax.dynamic_update_slice(buffer, block[None], (at, start, 0))
    l_all = put(l_all, here, z)
    up = down = here
    for step in range(1, 4):
        up, down = move(up, Z_UP), move(down, Z_DOWN)
        l_all = put(l_all, up, (z - step) % 8)
        l_all = put(l_all, down, (z + step) % 8)
    l_all = put(l_all, move(up[:512], Z_UP), (z + 4) % 8)
    l_all = put(l_all, move(down[512:], Z_DOWN), (z + 4) % 8, 512)

    across = jnp.concatenate([move(far[:512], Y_NEAR), move(near[512:], Y_FAR)], axis=0)
    a_all = jnp.stack([ainv, across, near, far])

    mine = (ylo != core).astype(jnp.int32)
    scalars = lambda which: jnp.stack([2 * which, yhi, x]).astype(jnp.int32)
    given = products(scalars(1 - mine), a_all, l_all, BF16)
    taken = move(given, CORE)
    kept = products(scalars(mine), a_all, l_all, F32)
    sums = [kept[j] + taken[j].astype(F32) for j in range(4)]

    first_up = move(sums[2][:512].astype(BF16), X_UP)
    first_down = move(sums[2][512:].astype(BF16), X_DOWN)
    one_up = jnp.concatenate([sums[1][:512] + first_up.astype(F32), sums[1][512:]], axis=0).astype(BF16)
    one_down = jnp.concatenate([sums[3][:512], sums[3][512:] + first_down.astype(F32)], axis=0).astype(BF16)
    total = sums[0] + move(one_up, X_UP).astype(F32) + move(one_down, X_DOWN).astype(F32)
    total = (-total).astype(BF16)
    total = jnp.where(ylo != core, move(total, HOME), total)
    inverse_column = jnp.where(flags, total, jnp.zeros((), BF16))

    terms = lax.dot_general(masked, inverse_column, (((0,), (0,)), ((), ())), preferred_element_type=F32)
    for pairs in (Y_NEAR, z_swap(1), z_swap(2), z_swap(4)):
        terms = terms.astype(BF16)
        terms = terms.astype(F32) + move(terms, pairs).astype(F32)
    return inverse_column[None], dinv - terms[None]


def solution(mesh):
    return jax.shard_map(
        body,
        mesh=mesh,
        in_specs=(P("prow", "pcol"), P("pcol", "prow", None), P("pcol", None, None), P(), P()),
        out_specs=(P("pcol", "prow", None), P("pcol", None, None)),
        check_vma=False,
    )
```

```python
import jax
import jax.numpy as jnp
from jax import lax
from jax.experimental import pallas as pl
from jax.experimental.pallas import tpu as pltpu
from jax.sharding import PartitionSpec as P

BS = 128
VMEM_MIB = 56
NZ, NY_LO, NX, NY_HI, NCORE = 8, 2, 4, 2, 2
F32, BF16 = jnp.float32, jnp.bfloat16
AXES = ("prow", "pcol")


def device_index(z, ylo, x, yhi, core):
    return (2 * z + ylo) * 16 + 4 * x + 2 * yhi + core


def permutation(target):
    pairs = []
    for z in range(NZ):
        for ylo in range(NY_LO):
            for x in range(NX):
                for yhi in range(NY_HI):
                    for core in range(NCORE):
                        to = target(z, ylo, x, yhi, core)
                        if to is not None:
                            pairs.append((device_index(z, ylo, x, yhi, core), device_index(*to)))
    return pairs


L_TURN = permutation(lambda z, l, x, q, c: (2 * ((x - z // 2) % 4) + z % 2, l, z // 2, q, c))
Z_UP = permutation(lambda z, l, x, q, c: ((z + 1) % 8, l, x, q, c))
Z_DOWN = permutation(lambda z, l, x, q, c: ((z - 1) % 8, l, x, q, c))
Y_NEAR = permutation(lambda z, l, x, q, c: (z, 1 - l, x, q, c))
Y_FAR = permutation(lambda z, l, x, q, c: (z, 1 - l, x, 1 - q, c))
CORE = permutation(lambda z, l, x, q, c: (z, l, x, q, 1 - c))
X_HOME = [permutation(lambda z, l, x, q, c, j=j: (z, c, (x + j) % 4, q, l)) for j in range(4)]


def swap(z_bits, ylo_bit):
    return permutation(lambda z, l, x, q, c: (z ^ z_bits, l ^ ylo_bit, x, q, c))


def move(value, pairs):
    return lax.ppermute(value, AXES, pairs)


def local_flags(ancestors, block_slot, row, column):
    own = lax.dynamic_index_in_dim(ancestors, column, 0, keepdims=False)
    numbers = jnp.arange(block_slot.shape[0], dtype=jnp.int32)
    used = jnp.any(own[:, None] == numbers[None, :], axis=0)
    slots = row * 8 + jnp.arange(8, dtype=jnp.int32)
    return jnp.any(used[None, :] & (block_slot[None, :] == slots[:, None]), axis=1)


L_STEPS = (0, -1, 1, -2, 2, -3, 3, 4, 4)


def product_kernel(scalars, *refs):
    own, across, near, far, l_refs, out = refs[0], refs[1:3], refs[3], refs[4], refs[5:14], refs[14]
    a_vmem, l_vmem, out_vmem, a_sem, l_sem, out_sem = refs[15:]
    z, yhi, which = scalars[0], scalars[1], scalars[2]

    def a_start(tile):
        rows = pl.ds(256 * tile, 256)
        sources = (
            (own.at[rows], across[tile // 2].at[pl.ds(256 * (tile % 2), 256)]),
            (near.at[rows], far.at[rows]),
        )
        for choice in range(2):
            @pl.when(which == choice)
            def _():
                for at in range(2):
                    target = a_vmem.at[rows, pl.ds(1024 * at, 1024)]
                    pltpu.make_async_copy(sources[choice][at], target, a_sem.at[tile]).start()

    def l_start(slots):
        for parity, sign in ((0, 1), (1, -1)):
            pairs = ((0, sign), (2 * sign, 3 * sign), (-sign, -2 * sign), (-3 * sign, 4))

            @pl.when(lax.rem(z, 2) == parity)
            def _():
                for slot in slots:
                    for step in pairs[slot]:
                        first = ((parity + step) % 2 ^ yhi) * 1024
                        for at in range(9):
                            if L_STEPS[at] == step:
                                rows = 512 if at >= 7 else 1024
                                start = pl.multiple_of(first + (512 if at == 8 else 0), 512)
                                target = l_vmem.at[slot, pl.ds(start, rows)]
                                pltpu.make_async_copy(l_refs[at], target, l_sem.at[slot]).start()

    a_start(0)
    l_start((0,))
    for tile in range(1, 4):
        a_start(tile)
    l_start((1, 2, 3))

    sign = 1 - 2 * lax.rem(z, 2)

    def multiply(slot, wait):
        pltpu.make_async_copy(l_vmem.at[slot], l_vmem.at[slot], l_sem.at[slot]).wait()
        for tile in range(4):
            rows = pl.ds(256 * tile, 256)
            if wait:
                pltpu.make_async_copy(a_vmem.at[rows], a_vmem.at[rows], a_sem.at[tile]).wait()
            total = jnp.dot(a_vmem[rows], l_vmem[slot], preferred_element_type=F32)
            out_vmem[slot, rows] = total.astype(BF16)
        shift = jnp.where(slot == 1, sign, jnp.where(slot == 2, -sign, jnp.where(slot == 3, 2, 0)))
        j = lax.rem(z // 2 + shift + 4, 4)
        pltpu.make_async_copy(out_vmem.at[slot], out.at[j], out_sem.at[slot]).start()

    multiply(0, True)

    @pl.loop(1, 4)
    def _(slot):
        multiply(slot, False)

    for slot in range(4):
        pltpu.make_async_copy(out_vmem.at[slot], out.at[slot], out_sem.at[slot]).wait()


def products(scalars, a_pieces, l_pieces):
    anywhere = pl.BlockSpec(memory_space=pl.ANY)
    return pl.pallas_call(
        product_kernel,
        in_specs=[pl.BlockSpec(memory_space=pltpu.SMEM)] + [anywhere] * 14,
        out_specs=anywhere,
        out_shape=jax.ShapeDtypeStruct((4, 1024, 256), BF16),
        scratch_shapes=[
            pltpu.VMEM((1024, 2048), BF16),
            pltpu.VMEM((4, 2048, 256), BF16),
            pltpu.VMEM((4, 1024, 256), BF16),
            pltpu.SemaphoreType.DMA((4,)),
            pltpu.SemaphoreType.DMA((4,)),
            pltpu.SemaphoreType.DMA((4,)),
        ],
        compiler_params=pltpu.CompilerParams(vmem_limit_bytes=VMEM_MIB * 2**20),
        cost_estimate=pl.CostEstimate(flops=2 * 1024 * 2048 * 1024, bytes_accessed=12 * 2**20, transcendentals=0),
    )(scalars, *a_pieces, *l_pieces)


def body(ainv, l_panels, dinv, ancestors, block_slot):
    row = lax.axis_index("prow")
    column = lax.axis_index("pcol")
    z, ylo = row // 2, row % 2
    x, yhi, core = column // 4, (column // 2) % 2, column % 2

    flags = jnp.repeat(local_flags(ancestors, block_slot, row, column), BS)[:, None]
    masked = jnp.where(flags, l_panels[0], jnp.zeros((), BF16))

    here = move(move(masked, X_HOME[0]), L_TURN)
    near = move(ainv, Y_NEAR)
    far = move(ainv, Y_FAR)

    l_pieces = [here]
    up = down = here
    for _ in range(2):
        up, down = move(up, Z_UP), move(down, Z_DOWN)
        l_pieces += [up, down]
    up, down, near, far = lax.optimization_barrier((up, down, near, far))
    across_top, across_bottom = move(far[:512], Y_NEAR), move(near[512:], Y_FAR)
    up, down = move(up, Z_UP), move(down, Z_DOWN)
    l_pieces += [up, down, move(up[:512], Z_UP), move(down[512:], Z_DOWN)]
    a_pieces = (ainv, across_top, across_bottom, near, far)

    mine = (ylo != core).astype(jnp.int32)
    give = jnp.stack([z, yhi, 1 - mine]).astype(jnp.int32)
    keep = jnp.stack([z, yhi, mine]).astype(jnp.int32)
    given = products(give, a_pieces, l_pieces)
    taken = move(given, CORE)
    kept = products(keep, a_pieces, l_pieces)
    sums = [(kept[j].astype(F32) + taken[j].astype(F32)).astype(BF16) for j in range(4)]

    total = sum(move(sums[j], X_HOME[j]).astype(F32) for j in (2, 1, 3, 0))
    inverse_column = jnp.where(flags, -total, jnp.zeros((), F32)).astype(BF16)

    terms = lax.dot_general(masked, inverse_column, (((0,), (0,)), ((), ())), preferred_element_type=F32)
    for pairs in (swap(0, 1), swap(1, 0), swap(2, 0), swap(4, 0)):
        terms = terms.astype(BF16)
        terms = terms.astype(F32) + move(terms, pairs).astype(F32)
    return inverse_column[None], dinv - terms[None]


def solution(mesh):
    return jax.shard_map(
        body,
        mesh=mesh,
        in_specs=(P("prow", "pcol"), P("pcol", "prow", None), P("pcol", None, None), P(), P()),
        out_specs=(P("pcol", "prow", None), P("pcol", None, None)),
        check_vma=False,
    )
```

```python
import jax
import jax.numpy as jnp
from jax import lax
from jax.experimental import pallas as pl
from jax.experimental.pallas import tpu as pltpu
from jax.sharding import PartitionSpec as P

BS = 128
VMEM_MIB = 56
NZ, NY_LO, NX, NY_HI, NCORE = 8, 2, 4, 2, 2
F32, BF16 = jnp.float32, jnp.bfloat16
AXES = ("prow", "pcol")


def device_index(z, ylo, x, yhi, core):
    return (2 * z + ylo) * 16 + 4 * x + 2 * yhi + core


def permutation(target):
    pairs = []
    for z in range(NZ):
        for ylo in range(NY_LO):
            for x in range(NX):
                for yhi in range(NY_HI):
                    for core in range(NCORE):
                        to = target(z, ylo, x, yhi, core)
                        if to is not None:
                            pairs.append((device_index(z, ylo, x, yhi, core), device_index(*to)))
    return pairs


L_TURN = permutation(lambda z, l, x, q, c: (2 * ((x - z // 2) % 4) + z % 2, l, z // 2, q, c))
CORE = permutation(lambda z, l, x, q, c: (z, l, x, q, 1 - c))
HOME = permutation(lambda z, l, x, q, c: (z, c, x, q, l))


def way(core):
    return 1 - 2 * core


Z_AHEAD = permutation(lambda z, l, x, q, c: ((z + way(c)) % 8, l, x, q, c))
Z_BACK = permutation(lambda z, l, x, q, c: ((z - way(c)) % 8, l, x, q, c))
Y_FIRST = permutation(lambda z, l, x, q, c: (z, 1 - l, x, q ^ c, c))
Y_SECOND = permutation(lambda z, l, x, q, c: (z, 1 - l, x, 1 - (q ^ c), c))
X_AHEAD = permutation(lambda z, l, x, q, c: (z, l, (x + way(c)) % 4, q, c))
X_AHEAD_HOME = permutation(lambda z, l, x, q, c: (z, c, (x + way(c)) % 4, q, l))
X_BACK_HOME = permutation(lambda z, l, x, q, c: (z, c, (x - way(c)) % 4, q, l))


def swap(z_bits, ylo_bit):
    return permutation(lambda z, l, x, q, c: (z ^ z_bits, l ^ ylo_bit, x, q, c))


def move(value, pairs):
    return lax.ppermute(value, AXES, pairs)


def local_flags(ancestors, block_slot, row, column):
    own = lax.dynamic_index_in_dim(ancestors, column, 0, keepdims=False)
    numbers = jnp.arange(block_slot.shape[0], dtype=jnp.int32)
    used = jnp.any(own[:, None] == numbers[None, :], axis=0)
    slots = row * 8 + jnp.arange(8, dtype=jnp.int32)
    return jnp.any(used[None, :] & (block_slot[None, :] == slots[:, None]), axis=1)


L_STEPS = (0, 1, -1, 2, -2, 3, -3, 4)


def product_kernel(scalars, *refs):
    own, across, first_y, second_y, l_refs, out = refs[0], refs[1], refs[2], refs[3], refs[4:12], refs[12]
    a_vmem, l_vmem, out_vmem, a_sem, l_sem, out_sem = refs[13:]
    z, half, which, side, order = scalars[0], scalars[1], scalars[2], scalars[3], scalars[4]

    def a_start(tile):
        rows = pl.ds(256 * tile, 256)
        for choice, sources in enumerate(((own, across), (first_y, second_y))):
            @pl.when(which == choice)
            def _():
                for at in range(2):
                    target = a_vmem.at[rows, pl.ds(1024 * at, 1024)]
                    pltpu.make_async_copy(sources[at].at[rows], target, a_sem.at[tile]).start()

    def l_start(slots):
        for parity, sign in ((0, -1), (1, 1)):
            pairs = ((0, sign), (2 * sign, 3 * sign), (-sign, -2 * sign), (-3 * sign, 4))

            @pl.when(side == parity)
            def _():
                for slot in slots:
                    for step in pairs[slot]:
                        start = pl.multiple_of((half ^ (step % 2)) * 1024, 1024)
                        target = l_vmem.at[slot, pl.ds(start, 1024)]
                        pltpu.make_async_copy(l_refs[L_STEPS.index(step)], target, l_sem.at[slot]).start()

    a_start(0)
    l_start((0,))
    for tile in range(1, 4):
        a_start(tile)
    l_start((1, 2, 3))

    sign = 1 - 2 * lax.rem(z, 2)

    def multiply(slot, wait):
        pltpu.make_async_copy(l_vmem.at[slot], l_vmem.at[slot], l_sem.at[slot]).wait()
        for tile in range(4):
            rows = pl.ds(256 * tile, 256)
            if wait:
                pltpu.make_async_copy(a_vmem.at[rows], a_vmem.at[rows], a_sem.at[tile]).wait()
            total = jnp.dot(a_vmem[rows], l_vmem[slot], preferred_element_type=F32)
            out_vmem[slot, rows] = total.astype(BF16)
        shift = jnp.where(slot == 1, sign, jnp.where(slot == 2, -sign, jnp.where(slot == 3, 2, 0)))
        j = lax.rem((z // 2 + shift + 4) * order, 4)
        pltpu.make_async_copy(out_vmem.at[slot], out.at[j], out_sem.at[slot]).start()

    multiply(0, True)

    @pl.loop(1, 4)
    def _(slot):
        multiply(slot, False)

    for slot in range(4):
        pltpu.make_async_copy(out_vmem.at[slot], out.at[slot], out_sem.at[slot]).wait()


def products(scalars, a_pieces, l_pieces):
    anywhere = pl.BlockSpec(memory_space=pl.ANY)
    return pl.pallas_call(
        product_kernel,
        in_specs=[pl.BlockSpec(memory_space=pltpu.SMEM)] + [anywhere] * 12,
        out_specs=anywhere,
        out_shape=jax.ShapeDtypeStruct((4, 1024, 256), BF16),
        scratch_shapes=[
            pltpu.VMEM((1024, 2048), BF16),
            pltpu.VMEM((4, 2048, 256), BF16),
            pltpu.VMEM((4, 1024, 256), BF16),
            pltpu.SemaphoreType.DMA((4,)),
            pltpu.SemaphoreType.DMA((4,)),
            pltpu.SemaphoreType.DMA((4,)),
        ],
        compiler_params=pltpu.CompilerParams(vmem_limit_bytes=VMEM_MIB * 2**20),
        cost_estimate=pl.CostEstimate(flops=2 * 1024 * 2048 * 1024, bytes_accessed=12 * 2**20, transcendentals=0),
    )(scalars, *a_pieces, *l_pieces)


def body(ainv, l_panels, dinv, ancestors, block_slot):
    row = lax.axis_index("prow")
    column = lax.axis_index("pcol")
    z, ylo = row // 2, row % 2
    x, yhi, core = column // 4, (column // 2) % 2, column % 2

    flags = jnp.repeat(local_flags(ancestors, block_slot, row, column), BS)[:, None]
    masked = jnp.where(flags, l_panels[0], jnp.zeros((), BF16))

    here = move(move(masked, HOME), L_TURN)
    first_y = move(ainv, Y_FIRST)
    second_y = move(ainv, Y_SECOND)

    l_pieces = [here]
    ahead = back = here
    for _ in range(2):
        ahead, back = move(ahead, Z_AHEAD), move(back, Z_BACK)
        l_pieces += [ahead, back]
    ahead, back, first_y, second_y = lax.optimization_barrier((ahead, back, first_y, second_y))
    across = move(second_y, Y_FIRST)
    ahead, back = move(ahead, Z_AHEAD), move(back, Z_BACK)
    l_pieces += [ahead, back, move(ahead, Z_AHEAD)]
    a_pieces = (ainv, across, first_y, second_y)

    mine = (ylo != core).astype(jnp.int32)

    def scalars(which, for_core):
        return jnp.stack([z, (z % 2) ^ yhi ^ (which & core), which, (z % 2) ^ core, 1 + 2 * for_core]).astype(jnp.int32)

    given = products(scalars(1 - mine, 1 - core), a_pieces, l_pieces)
    taken = move(given, CORE)
    kept = products(scalars(mine, core), a_pieces, l_pieces)
    sums = [kept[j].astype(F32) + taken[j].astype(F32) for j in range(4)]

    relayed = move(sums[2].astype(BF16), X_AHEAD)
    total = move(sums[3].astype(BF16), X_BACK_HOME).astype(F32) + move(sums[0].astype(BF16), HOME).astype(F32)
    total += move((sums[1] + relayed.astype(F32)).astype(BF16), X_AHEAD_HOME).astype(F32)
    inverse_column = jnp.where(flags, -total, jnp.zeros((), F32)).astype(BF16)

    terms = lax.dot_general(masked, inverse_column, (((0,), (0,)), ((), ())), preferred_element_type=F32)
    other = jnp.where(ylo == 0, terms[128:], terms[:128]).astype(BF16)
    half = jnp.where(ylo == 0, terms[:128], terms[128:]) + move(other, swap(0, 1)).astype(F32)
    for bit in (1, 2, 4):
        half = half.astype(BF16)
        half = half.astype(F32) + move(half, swap(bit, 0)).astype(F32)
    half = half.astype(BF16)
    other = move(half, swap(0, 1))
    terms = jnp.concatenate([jnp.where(ylo == 0, half, other), jnp.where(ylo == 0, other, half)], axis=0)
    return inverse_column[None], dinv - terms.astype(F32)[None]


def solution(mesh):
    return jax.shard_map(
        body,
        mesh=mesh,
        in_specs=(P("prow", "pcol"), P("pcol", "prow", None), P("pcol", None, None), P(), P()),
        out_specs=(P("pcol", "prow", None), P("pcol", None, None)),
        check_vma=False,
    )
```

```python
import functools

import jax
import jax.numpy as jnp
from jax import lax
from jax.experimental import pallas as pl
from jax.experimental.pallas import tpu as pltpu
from jax.sharding import PartitionSpec as P

BS = 128
VMEM_MIB = 56
NZ, NY_LO, NX, NY_HI, NCORE = 8, 2, 4, 2, 2
F32, BF16 = jnp.float32, jnp.bfloat16
AXES = ("prow", "pcol")


def device_index(z, ylo, x, yhi, core):
    return (2 * z + ylo) * 16 + 4 * x + 2 * yhi + core


def permutation(target):
    pairs = []
    for z in range(NZ):
        for ylo in range(NY_LO):
            for x in range(NX):
                for yhi in range(NY_HI):
                    for core in range(NCORE):
                        to = target(z, ylo, x, yhi, core)
                        if to is not None:
                            pairs.append((device_index(z, ylo, x, yhi, core), device_index(*to)))
    return pairs


L_TURN = permutation(lambda z, l, x, q, c: (2 * ((x - z // 2) % 4) + z % 2, l, z // 2, q, c))
CORE = permutation(lambda z, l, x, q, c: (z, l, x, q, 1 - c))
HOME = permutation(lambda z, l, x, q, c: (z, c, x, q, l))


def way(core):
    return 1 - 2 * core


Z_AHEAD = permutation(lambda z, l, x, q, c: ((z + way(c)) % 8, l, x, q, c))
Z_BACK = permutation(lambda z, l, x, q, c: ((z - way(c)) % 8, l, x, q, c))
Y_FIRST = permutation(lambda z, l, x, q, c: (z, 1 - l, x, q ^ c, c))
Y_SECOND = permutation(lambda z, l, x, q, c: (z, 1 - l, x, 1 - (q ^ c), c))
X_AHEAD = permutation(lambda z, l, x, q, c: (z, l, (x + way(c)) % 4, q, c))
X_AHEAD_HOME = permutation(lambda z, l, x, q, c: (z, c, (x + way(c)) % 4, q, l))
X_BACK_HOME = permutation(lambda z, l, x, q, c: (z, c, (x - way(c)) % 4, q, l))


def swap(z_bits, ylo_bit):
    return permutation(lambda z, l, x, q, c: (z ^ z_bits, l ^ ylo_bit, x, q, c))


def move(value, pairs):
    return lax.ppermute(value, AXES, pairs)


def local_flags(ancestors, block_slot, row, column):
    own = lax.dynamic_index_in_dim(ancestors, column, 0, keepdims=False)
    numbers = jnp.arange(block_slot.shape[0], dtype=jnp.int32)
    used = jnp.any(own[:, None] == numbers[None, :], axis=0)
    slots = row * 8 + jnp.arange(8, dtype=jnp.int32)
    return jnp.any(used[None, :] & (block_slot[None, :] == slots[:, None]), axis=1)


L_STEPS = (0, 1, -1, 2, -2, 3, -3, 4)


A_ROWS = 256


def product_kernel(early, scalars, *refs):
    if early:
        a_sets, l_refs, refs = (None, refs[0:2]), refs[2:9], refs[9:]
        outs, refs = refs[:2], refs[2:]
    else:
        a_sets, l_refs, refs = (refs[0:2], refs[2:4]), refs[4:12], refs[13:]
        outs, refs = refs[:1], refs[1:]
    a_vmem, l_vmem, out_vmem, a_sem, l_sem, out_sem = refs
    z, half, side, order, which = (scalars[at] for at in range(5))
    first_slot = 0 if early else 3 * which
    slots = 3 if early else 4

    def a_start(tile):
        rows = pl.ds(A_ROWS * tile, A_ROWS)
        for choice, sources in enumerate(a_sets):
            if sources is None:
                continue

            def start():
                for at in range(2):
                    target = a_vmem.at[rows, pl.ds(1024 * at, 1024)]
                    pltpu.make_async_copy(sources[at].at[rows], target, a_sem.at[tile]).start()

            if early:
                start()
            else:
                pl.when(which == choice)(start)

    def l_start(these):
        for parity, sign in ((0, -1), (1, 1)):
            pairs = ((0, sign), (2 * sign, 3 * sign), (-sign, -2 * sign), (-3 * sign, 4))

            @pl.when(side == parity)
            def _():
                for slot in these:
                    for step in pairs[slot]:
                        start = pl.multiple_of((half ^ (step % 2)) * 1024, 1024)
                        target = l_vmem.at[slot, pl.ds(start, 1024)]
                        pltpu.make_async_copy(l_refs[L_STEPS.index(step)], target, l_sem.at[slot]).start()

    a_start(0)
    if early:
        l_start((0,))
    else:
        pl.when(first_slot == 0)(lambda: l_start((0,)))
        pl.when(first_slot == 3)(lambda: l_start((3,)))
    for tile in range(1, 4):
        a_start(tile)
    if early:
        l_start((1, 2))
    else:
        pl.when(first_slot == 0)(lambda: l_start((1, 2, 3)))

    sign = 1 - 2 * lax.rem(z, 2)

    def multiply(slot, wait):
        pltpu.make_async_copy(l_vmem.at[slot], l_vmem.at[slot], l_sem.at[slot]).wait()
        for tile in range(4):
            rows = pl.ds(A_ROWS * tile, A_ROWS)
            if wait:
                pltpu.make_async_copy(a_vmem.at[rows], a_vmem.at[rows], a_sem.at[tile]).wait()
            total = jnp.dot(a_vmem[rows], l_vmem[slot], preferred_element_type=F32)
            out_vmem[slot, rows] = total.astype(BF16)
        shift = jnp.where(slot == 1, sign, jnp.where(slot == 2, -sign, jnp.where(slot == 3, 2, 0)))
        j = lax.rem((z // 2 + shift + 4) * order, 4)
        if early:
            for choice, out in enumerate(outs):
                @pl.when(which == choice)
                def _():
                    pltpu.make_async_copy(out_vmem.at[slot], out.at[j], out_sem.at[slot]).start()
        else:
            pltpu.make_async_copy(out_vmem.at[slot], outs[0].at[j], out_sem.at[slot]).start()

    def finish(slot):
        pltpu.make_async_copy(out_vmem.at[slot], outs[0].at[slot], out_sem.at[slot]).wait()

    def several():
        multiply(0, True)
        pl.loop(1, slots)(lambda slot: multiply(slot, False))
        for slot in range(slots):
            finish(slot)

    def last():
        multiply(3, True)
        finish(3)

    if early:
        several()
    else:
        pl.when(first_slot == 0)(several)
        pl.when(first_slot == 3)(last)


def product_call(early, scalars, *arrays):
    anywhere = pl.BlockSpec(memory_space=pl.ANY)
    block = jax.ShapeDtypeStruct((4, 1024, 256), BF16)
    slots = 3 if early else 2.5
    return pl.pallas_call(
        functools.partial(product_kernel, early),
        in_specs=[pl.BlockSpec(memory_space=pltpu.SMEM)] + [anywhere] * len(arrays),
        out_specs=(anywhere, anywhere) if early else anywhere,
        out_shape=(block, block) if early else block,
        scratch_shapes=[
            pltpu.VMEM((1024, 2048), BF16),
            pltpu.VMEM((4, 2048, 256), BF16),
            pltpu.VMEM((4, 1024, 256), BF16),
            pltpu.SemaphoreType.DMA((4,)),
            pltpu.SemaphoreType.DMA((4,)),
            pltpu.SemaphoreType.DMA((4,)),
        ],
        input_output_aliases={} if early else {len(arrays): 0},
        compiler_params=pltpu.CompilerParams(vmem_limit_bytes=VMEM_MIB * 2**20),
        cost_estimate=pl.CostEstimate(
            flops=int(slots * 2 * 1024 * 2048 * 256), bytes_accessed=10 * 2**20, transcendentals=0
        ),
    )(scalars, *arrays)


def products_early(scalars, a_pieces, l_pieces):
    return product_call(True, scalars, *a_pieces, *l_pieces)


def products(scalars, a_pieces, l_pieces, out):
    return product_call(False, scalars, *a_pieces, *l_pieces, out)


def body(ainv, l_panels, dinv, ancestors, block_slot):
    row = lax.axis_index("prow")
    column = lax.axis_index("pcol")
    z, ylo = row // 2, row % 2
    x, yhi, core = column // 4, (column // 2) % 2, column % 2

    flags = jnp.repeat(local_flags(ancestors, block_slot, row, column), BS)[:, None]
    masked = jnp.where(flags, l_panels[0], jnp.zeros((), BF16))

    here = move(move(masked, HOME), L_TURN)
    first_y = move(ainv, Y_FIRST)
    second_y = move(ainv, Y_SECOND)

    l_pieces = [here]
    ahead = back = here
    for _ in range(2):
        ahead, back = move(ahead, Z_AHEAD), move(back, Z_BACK)
        l_pieces += [ahead, back]
    ahead, back, first_y, second_y = lax.optimization_barrier((ahead, back, first_y, second_y))
    across = move(second_y, Y_FIRST)
    ahead, back = move(ahead, Z_AHEAD), move(back, Z_BACK)
    l_pieces += [ahead, back]

    given_is_other = (ylo == core).astype(jnp.int32)

    def scalars(other, for_core, last):
        half = (z % 2) ^ yhi ^ (other & core)
        return jnp.stack([z, half, (z % 2) ^ core, 1 + 2 * for_core, last]).astype(jnp.int32)

    for_core = jnp.where(given_is_other == 1, 1 - core, core)
    kept, given = products_early(scalars(1, for_core, given_is_other), (first_y, second_y), l_pieces)
    l_pieces.append(move(ahead, Z_AHEAD))
    a_pieces = (ainv, across, first_y, second_y)
    given = products(scalars(given_is_other, 1 - core, given_is_other), a_pieces, l_pieces, given)
    taken = move(given, CORE)
    kept = products(scalars(1 - given_is_other, core, 1 - given_is_other), a_pieces, l_pieces, kept)
    sums = [lax.optimization_barrier((kept[j].astype(F32) + taken[j].astype(F32)).astype(BF16)) for j in range(4)]

    relayed = move(sums[2], X_AHEAD)
    total = move(sums[3], X_BACK_HOME).astype(F32) + move(sums[0], HOME).astype(F32)
    total += move((sums[1].astype(F32) + relayed.astype(F32)).astype(BF16), X_AHEAD_HOME).astype(F32)
    inverse_column = jnp.where(flags, -total, jnp.zeros((), F32)).astype(BF16)

    terms = lax.dot_general(masked, inverse_column, (((0,), (0,)), ((), ())), preferred_element_type=F32)
    other = jnp.where(ylo == 0, terms[128:], terms[:128]).astype(BF16)
    half = jnp.where(ylo == 0, terms[:128], terms[128:]) + move(other, swap(0, 1)).astype(F32)
    for bits in (1, 2, 7):
        half = half.astype(BF16)
        half = half.astype(F32) + move(half, swap(bits, 0)).astype(F32)
    half = half.astype(BF16)
    other = move(half, swap(0, 1))
    terms = jnp.concatenate([jnp.where(ylo == 0, half, other), jnp.where(ylo == 0, other, half)], axis=0)
    return inverse_column[None], dinv - terms.astype(F32)[None]


def solution(mesh):
    return jax.shard_map(
        body,
        mesh=mesh,
        in_specs=(P("prow", "pcol"), P("pcol", "prow", None), P("pcol", None, None), P(), P()),
        out_specs=(P("pcol", "prow", None), P("pcol", None, None)),
        check_vma=False,
    )
```

```python
import functools

import jax
import jax.numpy as jnp
from jax import lax
from jax.experimental import pallas as pl
from jax.experimental.pallas import tpu as pltpu
from jax.sharding import PartitionSpec as P

BS = 128
VMEM_MIB = 32
NZ, NY_LO, NX, NY_HI, NCORE = 8, 2, 4, 2, 2
F32, BF16 = jnp.float32, jnp.bfloat16
AXES = ("prow", "pcol")


def device_index(z, ylo, x, yhi, core):
    return (2 * z + ylo) * 16 + 4 * x + 2 * yhi + core


def permutation(target):
    pairs = []
    for z in range(NZ):
        for ylo in range(NY_LO):
            for x in range(NX):
                for yhi in range(NY_HI):
                    for core in range(NCORE):
                        to = target(z, ylo, x, yhi, core)
                        if to is not None:
                            pairs.append((device_index(z, ylo, x, yhi, core), device_index(*to)))
    return pairs


L_TURN = permutation(lambda z, l, x, q, c: (2 * ((x - z // 2) % 4) + z % 2, l, z // 2, q, c))
CORE = permutation(lambda z, l, x, q, c: (z, l, x, q, 1 - c))
HOME = permutation(lambda z, l, x, q, c: (z, c, x, q, l))


def way(core):
    return 1 - 2 * core


Z_AHEAD = permutation(lambda z, l, x, q, c: ((z + way(c)) % 8, l, x, q, c))
Z_BACK = permutation(lambda z, l, x, q, c: ((z - way(c)) % 8, l, x, q, c))
Y_FIRST = permutation(lambda z, l, x, q, c: (z, 1 - l, x, q ^ c, c))
Y_SECOND = permutation(lambda z, l, x, q, c: (z, 1 - l, x, 1 - (q ^ c), c))
X_AHEAD = permutation(lambda z, l, x, q, c: (z, l, (x + way(c)) % 4, q, c))
X_AHEAD_HOME = permutation(lambda z, l, x, q, c: (z, c, (x + way(c)) % 4, q, l))
X_BACK_HOME = permutation(lambda z, l, x, q, c: (z, c, (x - way(c)) % 4, q, l))


def swap(z_bits, ylo_bit):
    return permutation(lambda z, l, x, q, c: (z ^ z_bits, l ^ ylo_bit, x, q, c))


def move(value, pairs):
    return lax.ppermute(value, AXES, pairs)


def local_flags(ancestors, block_slot, row, column):
    own = lax.dynamic_index_in_dim(ancestors, column, 0, keepdims=False)
    numbers = jnp.arange(block_slot.shape[0], dtype=jnp.int32)
    used = jnp.any(own[:, None] == numbers[None, :], axis=0)
    slots = row * 8 + jnp.arange(8, dtype=jnp.int32)
    return jnp.any(used[None, :] & (block_slot[None, :] == slots[:, None]), axis=1)


L_STEPS = (0, 1, -1, 2, -2, 3, -3, 4)


A_ROWS = 256


def product_kernel(early, scalars, *refs):
    if early:
        other_refs, l_refs, refs = refs[0:2], refs[2:9], refs[9:]
    else:
        own_refs, other_refs, l_refs, refs = refs[0:2], refs[2:4], refs[4:12], refs[14:]
    outs, (own_vmem, other_vmem, l_vmem, out_vmem, own_sem, other_sem, l_sem, out_sem) = refs[:2], refs[2:]
    z, half, side, own_order, other_order, other_out, core = (scalars[at] for at in range(7))

    def a_start(sources, target, sem, flip, tile):
        rows = pl.ds(A_ROWS * tile, A_ROWS)
        for at, source in enumerate(sources):
            columns = pl.ds(pl.multiple_of((at ^ flip) * 1024, 1024), 1024)
            pltpu.make_async_copy(source.at[rows], target.at[rows, columns], sem.at[tile]).start()

    def l_start(these):
        for parity, sign in ((0, -1), (1, 1)):
            pairs = ((0, sign), (2 * sign, 3 * sign), (-sign, -2 * sign), (-3 * sign, 4))

            @pl.when(side == parity)
            def _():
                for slot in these:
                    for step in pairs[slot]:
                        start = pl.multiple_of((half ^ (step % 2)) * 1024, 1024)
                        target = l_vmem.at[slot, pl.ds(start, 1024)]
                        pltpu.make_async_copy(l_refs[L_STEPS.index(step)], target, l_sem.at[slot]).start()

    def own_start(tile):
        a_start(own_refs, own_vmem, own_sem, 0, tile)

    def other_start(tile):
        a_start(other_refs, other_vmem, other_sem, core, tile)

    first_start = other_start if early else own_start
    first_start(0)
    l_start((0,))
    for tile in range(1, 4):
        first_start(tile)
    l_start((1, 2) if early else (1, 2, 3))
    if not early:
        for tile in range(4):
            other_start(tile)

    sign = 1 - 2 * lax.rem(z, 2)

    def multiply(a_vmem, a_sem, slot, result, order, which, wait_l=True):
        if wait_l:
            pltpu.make_async_copy(l_vmem.at[slot], l_vmem.at[slot], l_sem.at[slot]).wait()
        for tile in range(4):
            rows = pl.ds(A_ROWS * tile, A_ROWS)
            if a_sem is not None:
                pltpu.make_async_copy(a_vmem.at[rows], a_vmem.at[rows], a_sem.at[tile]).wait()
            total = jnp.dot(a_vmem[rows], l_vmem[slot], preferred_element_type=F32)
            out_vmem[result, rows] = total.astype(BF16)
        shift = jnp.where(slot == 1, sign, jnp.where(slot == 2, -sign, jnp.where(slot == 3, 2, 0)))
        j = lax.rem((z // 2 + shift + 4) * order, 4)
        for choice, out in enumerate(outs):
            @pl.when(which == choice)
            def _():
                pltpu.make_async_copy(out_vmem.at[result], out.at[j], out_sem.at[result]).start()

    if early:
        multiply(other_vmem, other_sem, 0, 0, other_order, other_out)
        pl.loop(1, 3)(lambda slot: multiply(other_vmem, None, slot, slot, other_order, other_out))
    else:
        multiply(own_vmem, own_sem, 0, 0, own_order, 1 - other_out)
        pl.loop(1, 4)(lambda slot: multiply(own_vmem, None, slot, slot, own_order, 1 - other_out))
        multiply(other_vmem, other_sem, 3, 4, other_order, other_out, wait_l=False)
    for result in range(3 if early else 5):
        pltpu.make_async_copy(out_vmem.at[result], outs[0].at[0], out_sem.at[result]).wait()


def product_call(early, scalars, *arrays):
    anywhere = pl.BlockSpec(memory_space=pl.ANY)
    block = jax.ShapeDtypeStruct((4, 1024, 256), BF16)
    slots = 3 if early else 5
    return pl.pallas_call(
        functools.partial(product_kernel, early),
        in_specs=[pl.BlockSpec(memory_space=pltpu.SMEM)] + [anywhere] * len(arrays),
        out_specs=(anywhere, anywhere),
        out_shape=(block, block),
        scratch_shapes=[
            pltpu.VMEM((1024, 2048), BF16),
            pltpu.VMEM((1024, 2048), BF16),
            pltpu.VMEM((4, 2048, 256), BF16),
            pltpu.VMEM((5, 1024, 256), BF16),
            pltpu.SemaphoreType.DMA((4,)),
            pltpu.SemaphoreType.DMA((4,)),
            pltpu.SemaphoreType.DMA((4,)),
            pltpu.SemaphoreType.DMA((5,)),
        ],
        input_output_aliases={} if early else {len(arrays) - 1: 0, len(arrays): 1},
        compiler_params=pltpu.CompilerParams(vmem_limit_bytes=VMEM_MIB * 2**20),
        cost_estimate=pl.CostEstimate(
            flops=slots * 2 * 1024 * 2048 * 256, bytes_accessed=10 * 2**20, transcendentals=0
        ),
    )(scalars, *arrays)


def products_early(scalars, a_pieces, l_pieces):
    return product_call(True, scalars, *a_pieces, *l_pieces)


def products(scalars, a_pieces, l_pieces, outs):
    return product_call(False, scalars, *a_pieces, *l_pieces, *outs)


def body(ainv, l_panels, dinv, ancestors, block_slot):
    row = lax.axis_index("prow")
    column = lax.axis_index("pcol")
    z, ylo = row // 2, row % 2
    x, yhi, core = column // 4, (column // 2) % 2, column % 2

    flags = jnp.repeat(local_flags(ancestors, block_slot, row, column), BS)[:, None]
    masked = jnp.where(flags, l_panels[0], jnp.zeros((), BF16))

    here = move(move(masked, HOME), L_TURN)
    first_y = move(ainv, Y_FIRST)
    second_y = move(ainv, Y_SECOND)

    l_pieces = [here]
    ahead = back = here
    for _ in range(2):
        ahead, back = move(ahead, Z_AHEAD), move(back, Z_BACK)
        l_pieces += [ahead, back]
    ahead, back, first_y, second_y = lax.optimization_barrier((ahead, back, first_y, second_y))
    across = move(second_y, Y_FIRST)
    ahead, back = move(ahead, Z_AHEAD), move(back, Z_BACK)
    l_pieces += [ahead, back]

    given_is_other = (ylo == core).astype(jnp.int32)
    own_core, other_core = jnp.where(given_is_other == 1, jnp.stack([core, 1 - core]), jnp.stack([1 - core, core]))
    scalars = [z, (z % 2) ^ yhi, (z % 2) ^ core, 1 + 2 * own_core, 1 + 2 * other_core, given_is_other, core]
    scalars = jnp.stack(scalars).astype(jnp.int32)
    outs = products_early(scalars, (first_y, second_y), l_pieces)
    l_pieces.append(move(ahead, Z_AHEAD))
    kept, given = products(scalars, (ainv, across, first_y, second_y), l_pieces, outs)
    taken = move(given, CORE)

    def block_sum(j):
        return (kept[j].astype(F32) + taken[j].astype(F32)).astype(BF16)

    sum_2, kept, taken = lax.optimization_barrier((block_sum(2), kept, taken))
    sum_3, sum_0, kept, taken = lax.optimization_barrier((block_sum(3), block_sum(0), kept, taken))
    sum_1 = lax.optimization_barrier(block_sum(1))

    relayed = move(sum_2, X_AHEAD)
    total = move(sum_3, X_BACK_HOME).astype(F32) + move(sum_0, HOME).astype(F32)
    total += move((sum_1.astype(F32) + relayed.astype(F32)).astype(BF16), X_AHEAD_HOME).astype(F32)
    inverse_column = jnp.where(flags, -total, jnp.zeros((), F32)).astype(BF16)

    terms = lax.dot_general(masked, inverse_column, (((0,), (0,)), ((), ())), preferred_element_type=F32)
    other = jnp.where(ylo == 0, terms[128:], terms[:128]).astype(BF16)
    half = jnp.where(ylo == 0, terms[:128], terms[128:]) + move(other, swap(0, 1)).astype(F32)
    for bits in (1, 2, 7):
        half = half.astype(BF16)
        half = half.astype(F32) + move(half, swap(bits, 0)).astype(F32)
    half = half.astype(BF16)
    other = move(half, swap(0, 1))
    terms = jnp.concatenate([jnp.where(ylo == 0, half, other), jnp.where(ylo == 0, other, half)], axis=0)
    return inverse_column[None], dinv - terms.astype(F32)[None]


def solution(mesh):
    return jax.shard_map(
        body,
        mesh=mesh,
        in_specs=(P("prow", "pcol"), P("pcol", "prow", None), P("pcol", None, None), P(), P()),
        out_specs=(P("pcol", "prow", None), P("pcol", None, None)),
        check_vma=False,
    )
```

```python
import functools

import jax
import jax.numpy as jnp
from jax import lax
from jax.experimental import pallas as pl
from jax.experimental.pallas import tpu as pltpu
from jax.sharding import PartitionSpec as P

BS = 128
VMEM_MIB = 32
NZ, NY_LO, NX, NY_HI, NCORE = 8, 2, 4, 2, 2
F32, BF16 = jnp.float32, jnp.bfloat16
AXES = ("prow", "pcol")


def device_index(z, ylo, x, yhi, core):
    return (2 * z + ylo) * 16 + 4 * x + 2 * yhi + core


def permutation(target):
    pairs = []
    for z in range(NZ):
        for ylo in range(NY_LO):
            for x in range(NX):
                for yhi in range(NY_HI):
                    for core in range(NCORE):
                        to = target(z, ylo, x, yhi, core)
                        if to is not None:
                            pairs.append((device_index(z, ylo, x, yhi, core), device_index(*to)))
    return pairs


L_TURN = permutation(lambda z, l, x, q, c: (2 * ((x - z // 2) % 4) + z % 2, l, z // 2, q, c))
CORE = permutation(lambda z, l, x, q, c: (z, l, x, q, 1 - c))
HOME = permutation(lambda z, l, x, q, c: (z, c, x, q, l))


def way(core):
    return 1 - 2 * core


Z_AHEAD = permutation(lambda z, l, x, q, c: ((z + way(c)) % 8, l, x, q, c))
Z_BACK = permutation(lambda z, l, x, q, c: ((z - way(c)) % 8, l, x, q, c))
Y_FIRST = permutation(lambda z, l, x, q, c: (z, 1 - l, x, q ^ c, c))
Y_SECOND = permutation(lambda z, l, x, q, c: (z, 1 - l, x, 1 - (q ^ c), c))
X_AHEAD = permutation(lambda z, l, x, q, c: (z, l, (x + way(c)) % 4, q, c))
X_AHEAD_HOME = permutation(lambda z, l, x, q, c: (z, c, (x + way(c)) % 4, q, l))
X_BACK_HOME = permutation(lambda z, l, x, q, c: (z, c, (x - way(c)) % 4, q, l))


def swap(z_bits, ylo_bit):
    return permutation(lambda z, l, x, q, c: (z ^ z_bits, l ^ ylo_bit, x, q, c))


def move(value, pairs):
    return lax.ppermute(value, AXES, pairs)


def local_flags(ancestors, block_slot, row, column):
    own = lax.dynamic_index_in_dim(ancestors, column, 0, keepdims=False)
    numbers = jnp.arange(block_slot.shape[0], dtype=jnp.int32)
    used = jnp.any(own[:, None] == numbers[None, :], axis=0)
    slots = row * 8 + jnp.arange(8, dtype=jnp.int32)
    return jnp.any(used[None, :] & (block_slot[None, :] == slots[:, None]), axis=1)


L_STEPS = (0, 1, -1, 2, -2, 3, -3, 4)


A_ROWS = 256


def product_kernel(early, scalars, *refs):
    if early:
        other_refs, l_refs, refs = refs[0:2], refs[2:9], refs[9:]
    else:
        own_refs, other_refs, l_refs, refs = refs[0:2], refs[2:4], refs[4:12], refs[14:]
    outs, (own_vmem, other_vmem, l_vmem, out_vmem, own_sem, other_sem, l_sem, out_sem) = refs[:2], refs[2:]
    z, half, side, own_order, other_order, other_out, core = (scalars[at] for at in range(7))

    def a_start(sources, target, sem, flip, tile):
        rows = pl.ds(A_ROWS * tile, A_ROWS)
        for at, source in enumerate(sources):
            columns = pl.ds(pl.multiple_of((at ^ flip) * 1024, 1024), 1024)
            pltpu.make_async_copy(source.at[rows], target.at[rows, columns], sem.at[tile]).start()

    def l_start(these):
        for parity, sign in ((0, -1), (1, 1)):
            pairs = ((0, sign), (2 * sign, 3 * sign), (-sign, -2 * sign), (-3 * sign, 4))

            @pl.when(side == parity)
            def _():
                for slot in these:
                    for step in pairs[slot]:
                        start = pl.multiple_of((half ^ (step % 2)) * 1024, 1024)
                        target = l_vmem.at[slot, pl.ds(start, 1024)]
                        pltpu.make_async_copy(l_refs[L_STEPS.index(step)], target, l_sem.at[slot]).start()

    def own_start(tile):
        a_start(own_refs, own_vmem, own_sem, 0, tile)

    def other_start(tile):
        a_start(other_refs, other_vmem, other_sem, core, tile)

    first_start = other_start if early else own_start
    first_start(0)
    l_start((0,))
    for tile in range(1, 4):
        first_start(tile)
    l_start((1, 2) if early else (1, 2, 3))
    if not early:
        for tile in range(4):
            other_start(tile)

    sign = 1 - 2 * lax.rem(z, 2)

    def multiply(a_vmem, a_sem, slot, result, order, which, wait_l=True):
        if wait_l:
            pltpu.make_async_copy(l_vmem.at[slot], l_vmem.at[slot], l_sem.at[slot]).wait()
        for tile in range(4):
            rows = pl.ds(A_ROWS * tile, A_ROWS)
            if a_sem is not None:
                pltpu.make_async_copy(a_vmem.at[rows], a_vmem.at[rows], a_sem.at[tile]).wait()
            total = jnp.dot(a_vmem[rows], l_vmem[slot], preferred_element_type=F32)
            out_vmem[result, rows] = total.astype(BF16)
        shift = (0, sign, -sign, 2)[slot]
        j = lax.rem((z // 2 + shift + 4) * order, 4)
        for choice, out in enumerate(outs):
            @pl.when(which == choice)
            def _():
                pltpu.make_async_copy(out_vmem.at[result], out.at[j], out_sem.at[result]).start()

    if early:
        multiply(other_vmem, other_sem, 0, 0, other_order, other_out)
        for slot in range(1, 3):
            multiply(other_vmem, None, slot, slot, other_order, other_out)
    else:
        multiply(own_vmem, own_sem, 0, 0, own_order, 1 - other_out)
        for slot in range(1, 4):
            multiply(own_vmem, None, slot, slot, own_order, 1 - other_out)
        multiply(other_vmem, other_sem, 3, 4, other_order, other_out, wait_l=False)
    for result in range(3 if early else 5):
        pltpu.make_async_copy(out_vmem.at[result], outs[0].at[0], out_sem.at[result]).wait()


def product_call(early, scalars, *arrays):
    anywhere = pl.BlockSpec(memory_space=pl.ANY)
    block = jax.ShapeDtypeStruct((4, 1024, 256), BF16)
    slots = 3 if early else 5
    return pl.pallas_call(
        functools.partial(product_kernel, early),
        in_specs=[pl.BlockSpec(memory_space=pltpu.SMEM)] + [anywhere] * len(arrays),
        out_specs=(anywhere, anywhere),
        out_shape=(block, block),
        scratch_shapes=[
            pltpu.VMEM((1024, 2048), BF16),
            pltpu.VMEM((1024, 2048), BF16),
            pltpu.VMEM((4, 2048, 256), BF16),
            pltpu.VMEM((5, 1024, 256), BF16),
            pltpu.SemaphoreType.DMA((4,)),
            pltpu.SemaphoreType.DMA((4,)),
            pltpu.SemaphoreType.DMA((4,)),
            pltpu.SemaphoreType.DMA((5,)),
        ],
        input_output_aliases={} if early else {len(arrays) - 1: 0, len(arrays): 1},
        compiler_params=pltpu.CompilerParams(vmem_limit_bytes=VMEM_MIB * 2**20),
        cost_estimate=pl.CostEstimate(
            flops=slots * 2 * 1024 * 2048 * 256, bytes_accessed=10 * 2**20, transcendentals=0
        ),
    )(scalars, *arrays)


def products_early(scalars, a_pieces, l_pieces):
    return product_call(True, scalars, *a_pieces, *l_pieces)


def products(scalars, a_pieces, l_pieces, outs):
    return product_call(False, scalars, *a_pieces, *l_pieces, *outs)


def body(ainv, l_panels, dinv, ancestors, block_slot):
    row = lax.axis_index("prow")
    column = lax.axis_index("pcol")
    z, ylo = row // 2, row % 2
    x, yhi, core = column // 4, (column // 2) % 2, column % 2

    flags = jnp.repeat(local_flags(ancestors, block_slot, row, column), BS)[:, None]
    masked = jnp.where(flags, l_panels[0], jnp.zeros((), BF16))

    here = move(move(masked, HOME), L_TURN)
    first_y = move(ainv, Y_FIRST)
    second_y = move(ainv, Y_SECOND)

    l_pieces = [here]
    ahead = back = here
    for _ in range(2):
        ahead, back = move(ahead, Z_AHEAD), move(back, Z_BACK)
        l_pieces += [ahead, back]
    ahead, back, first_y, second_y = lax.optimization_barrier((ahead, back, first_y, second_y))
    across = move(second_y, Y_FIRST)
    ahead, back = move(ahead, Z_AHEAD), move(back, Z_BACK)
    l_pieces += [ahead, back]

    given_is_other = (ylo == core).astype(jnp.int32)
    own_core, other_core = jnp.where(given_is_other == 1, jnp.stack([core, 1 - core]), jnp.stack([1 - core, core]))
    scalars = [z, (z % 2) ^ yhi, (z % 2) ^ core, 1 + 2 * own_core, 1 + 2 * other_core, given_is_other, core]
    scalars = jnp.stack(scalars).astype(jnp.int32)
    outs = products_early(scalars, (first_y, second_y), l_pieces)
    l_pieces.append(move(ahead, Z_AHEAD))
    kept, given = products(scalars, (ainv, across, first_y, second_y), l_pieces, outs)
    taken = move(given, CORE)

    def block_sum(j):
        return (kept[j].astype(F32) + taken[j].astype(F32)).astype(BF16)

    sum_2, kept, taken = lax.optimization_barrier((block_sum(2), kept, taken))
    sum_3, sum_0, kept, taken = lax.optimization_barrier((block_sum(3), block_sum(0), kept, taken))
    sum_1 = lax.optimization_barrier(block_sum(1))

    relayed = move(sum_2, X_AHEAD)
    total = move(sum_3, X_BACK_HOME).astype(F32) + move(sum_0, HOME).astype(F32)
    total += move((sum_1.astype(F32) + relayed.astype(F32)).astype(BF16), X_AHEAD_HOME).astype(F32)
    inverse_column = jnp.where(flags, -total, jnp.zeros((), F32)).astype(BF16)

    terms = lax.dot_general(masked, inverse_column, (((0,), (0,)), ((), ())), preferred_element_type=F32)
    other = jnp.where(ylo == 0, terms[128:], terms[:128]).astype(BF16)
    half = jnp.where(ylo == 0, terms[:128], terms[128:]) + move(other, swap(0, 1)).astype(F32)
    for bits in (1, 2, 7):
        half = half.astype(BF16)
        half = half.astype(F32) + move(half, swap(bits, 0)).astype(F32)
    half = half.astype(BF16)
    other = move(half, swap(0, 1))
    terms = jnp.concatenate([jnp.where(ylo == 0, half, other), jnp.where(ylo == 0, other, half)], axis=0)
    return inverse_column[None], dinv - terms.astype(F32)[None]


def solution(mesh):
    return jax.shard_map(
        body,
        mesh=mesh,
        in_specs=(P("prow", "pcol"), P("pcol", "prow", None), P("pcol", None, None), P(), P()),
        out_specs=(P("pcol", "prow", None), P("pcol", None, None)),
        check_vma=False,
    )
```
